32 devices in a mesh: row: 4 (over x, core), col: 8 (over z, y).
Axes of the slice: x: 2, y: 2, z: 4, core: 2. Of those that a mesh axis runs over, the one named last changes fastest.
Arguments:
- derivs: bfloat16 [256, 65536], P(('row', 'col')), may hold values from -15 to 15, as said below
- energy_derivs: bfloat16 [256, 65536], P(('row', 'col')), may hold values from -15 to 15, as said below
- energies: float32 [256], P(('row', 'col')), may hold values from -30 to -10, as said below
Outputs:
- correlation: float32 [4096, 65536], P('row', 'col')
- hamiltonian: float32 [4096, 65536], P('row', 'col')
The draws below stay inside these ranges and needn't reach their ends.
Inputs may be any that keep to these rules, and one draw needn't show every extreme that they name: `derivs`: finite values. `energy_derivs`: finite values. `energies`: finite values.
All inputs are finite; a program needn't handle non-finite values.
Results may differ from the reference program's by a relative error of at most 0.0041.
Values may be sent and summed in bfloat16 or wider, within the bound.
No kernel may reach another device: no remote copies, remote signals or barrier semaphores. Data moves between devices by JAX's collectives and lax.ppermute only.
A program may use at most 128 MiB of HBM per device.

```python
import math
import jax
import jax.numpy as jnp
from jax import lax

P_SIZE = 65536
SLAB = 4096
NS = 256


def trend_weights():
    positions = jnp.arange(NS, dtype=jnp.float32)
    return 0.5 + positions / (NS - 1)


def sample_block(seed_key):
    keys = jax.random.split(seed_key, 3)
    scales = jnp.exp(jax.random.uniform(keys[0], (P_SIZE,), jnp.float32, math.log(0.3), math.log(3.0)))
    offsets = jax.random.uniform(keys[1], (P_SIZE,), jnp.float32, -1.5, 1.5)
    noise = jnp.clip(jax.random.normal(keys[2], (NS, P_SIZE), jnp.float32), -4.0, 4.0)
    values = trend_weights()[:, None] * offsets[None, :] + noise * scales[None, :]
    return values.astype(jnp.bfloat16)


def draw_derivs(key, part):
    return sample_block(jax.random.fold_in(key, 101))


def draw_energy_derivs(key, part):
    return sample_block(jax.random.fold_in(key, 202))


def draw_energies(key, part):
    seed_key = jax.random.fold_in(key, 303)
    noise = jnp.clip(jax.random.normal(seed_key, (NS,), jnp.float32), -4.0, 4.0)
    return -20.0 + 3.0 * trend_weights() + noise


def setup_inputs(seed: int = 0) -> dict:
    key_list = jax.random.split(jax.random.key(seed), 4)
    derivs = draw_derivs(jax.random.fold_in(key_list[3], 71), 0)
    energy_derivs = draw_energy_derivs(jax.random.fold_in(key_list[3], 71), 0)
    energies = draw_energies(jax.random.fold_in(key_list[3], 71), 0)
    return {"derivs": derivs, "energy_derivs": energy_derivs, "energies": energies}


def reference(derivs, energy_derivs, energies):
    total_count = derivs.shape[0]
    derivs_full = derivs.astype(jnp.float32)
    grads_full = energy_derivs.astype(jnp.float32)
    mean_derivs = jnp.sum(derivs_full, axis=0) / total_count
    mean_grads = jnp.sum(grads_full, axis=0) / total_count
    mean_energy = jnp.sum(energies) / total_count
    offsets = derivs_full - mean_derivs[None, :]
    centred = offsets.astype(jnp.bfloat16)
    energy_term = ((energies - mean_energy)[:, None] * offsets + (grads_full - mean_grads[None, :])).astype(jnp.bfloat16)
    row_block = centred[:, :SLAB]
    width = min(P_SIZE, 4096)
    blocks = P_SIZE // width
    centred_blocks = centred.reshape(total_count, blocks, width).transpose(1, 0, 2)
    term_blocks = energy_term.reshape(total_count, blocks, width).transpose(1, 0, 2)

    def one_block(pair_blocks):
        left = lax.dot_general(row_block, pair_blocks[0], (((0,), (0,)), ((), ())), preferred_element_type=jnp.float32)
        right = lax.dot_general(row_block, pair_blocks[1], (((0,), (0,)), ((), ())), preferred_element_type=jnp.float32)
        return left, right

    over_blocks, hamil_blocks = lax.map(one_block, (centred_blocks, term_blocks))
    correlation = over_blocks.transpose(1, 0, 2).reshape(SLAB, P_SIZE) / total_count
    hamiltonian = hamil_blocks.transpose(1, 0, 2).reshape(SLAB, P_SIZE) / total_count
    return correlation, hamiltonian
```

```python
import functools
import jax
import jax.numpy as jnp
from jax import lax
from jax.experimental import pallas as pl
from jax.experimental.pallas import tpu as pltpu
from jax.sharding import PartitionSpec as P

VMEM_BYTES = 40 * 1024 * 1024
LANES = 128
SHARES = (4, 3, 1)


def averaged(values, count):
    if count & (count - 1) == 0:
        return values * (1.0 / count)
    return values / count


def prepare_kernel(first_half, second_half, energy, row_out, shift_out):
    count = energy.shape[0]
    half = first_half.shape[1]
    for place, source in enumerate((first_half, second_half)):
        raw = source[...].astype(jnp.float32)
        centred = raw - averaged(jnp.sum(raw, axis=0, keepdims=True), count)
        row_out[place * half : (place + 1) * half, :] = centred.T.astype(jnp.bfloat16)
    parts = energy[...].astype(jnp.float32)
    value = (parts[:, 0:1] + parts[:, 1:2]) + parts[:, 2:3]
    shift = value - averaged(jnp.sum(value, axis=0, keepdims=True), count)
    shift_out[...] = jnp.broadcast_to(shift, shift_out.shape)


def prepare(first_half, second_half, energy):
    count, half = first_half.shape
    return pl.pallas_call(
        prepare_kernel,
        out_shape=(
            jax.ShapeDtypeStruct((2 * half, count), jnp.bfloat16),
            jax.ShapeDtypeStruct((count, LANES), jnp.float32),
        ),
        compiler_params=pltpu.CompilerParams(vmem_limit_bytes=VMEM_BYTES),
        cost_estimate=pl.CostEstimate(flops=4 * half * count, bytes_accessed=8 * half * count, transcendentals=0),
    )(first_half, second_half, energy)


def chunk_kernel(row_ref, shift_ref, *refs, pieces):
    derivs = refs[:pieces]
    grads = refs[pieces : 2 * pieces]
    correlation, hamiltonian = refs[-2:]
    count = row_ref.shape[1]
    raw = jnp.concatenate([piece[...] for piece in derivs], axis=0).astype(jnp.float32)
    raw_grads = jnp.concatenate([piece[...] for piece in grads], axis=0).astype(jnp.float32)
    offsets = raw - averaged(jnp.sum(raw, axis=0, keepdims=True), count)
    grad_offsets = raw_grads - averaged(jnp.sum(raw_grads, axis=0, keepdims=True), count)
    centred = offsets.astype(jnp.bfloat16)
    term = (shift_ref[:, 0:1] * offsets + grad_offsets).astype(jnp.bfloat16)
    rows = row_ref[...]
    correlation[...] = averaged(jnp.dot(rows, centred, preferred_element_type=jnp.float32), count)
    hamiltonian[...] = averaged(jnp.dot(rows, term, preferred_element_type=jnp.float32), count)


def chunk_products(rows, shift, pieces, start, width, block, total_width, earlier):
    steps = width // block
    first = start // block
    n_rows = rows.shape[0]
    specs = [pl.BlockSpec(rows.shape, lambda j: (0, 0)), pl.BlockSpec(shift.shape, lambda j: (0, 0))]
    for offset in (0, steps):
        specs += [pl.BlockSpec((p.shape[0], block), lambda j, o=offset: (0, j + o)) for p in pieces]
    operands = [rows, shift, *pieces, *pieces]
    aliases = {}
    if earlier is not None:
        aliases = {len(operands): 0, len(operands) + 1: 1}
        operands += list(earlier)
        specs += [pl.BlockSpec(memory_space=pl.ANY)] * 2
    return pl.pallas_call(
        functools.partial(chunk_kernel, pieces=len(pieces)),
        grid=(steps,),
        in_specs=specs,
        out_specs=[pl.BlockSpec((n_rows, block), lambda j: (0, j + first))] * 2,
        out_shape=[jax.ShapeDtypeStruct((n_rows, total_width), jnp.float32)] * 2,
        input_output_aliases=aliases,
        compiler_params=pltpu.CompilerParams(vmem_limit_bytes=VMEM_BYTES),
        cost_estimate=pl.CostEstimate(
            flops=4 * n_rows * width * rows.shape[1], bytes_accessed=8 * n_rows * width, transcendentals=0
        ),
    )(*operands)


def energy_parts(energies):
    high = lax.reduce_precision(energies, 8, 7)
    rest = energies - high
    middle = lax.reduce_precision(rest, 8, 7)
    low = rest - middle
    parts = jnp.stack((high, middle, low), axis=1).astype(jnp.bfloat16)
    return jnp.pad(parts, ((0, 0), (0, LANES - 3)))


def across(value, axis, distance):
    size = lax.axis_size(axis)
    return lax.ppermute(value, axis, [(i, i ^ distance) for i in range(size)])


def body(derivs, energy_derivs, energies):
    row_count = lax.axis_size("row")
    col_count = lax.axis_size("col")
    local = derivs.shape[0]
    total_width = derivs.shape[1] // col_count
    slab = derivs.shape[1] // 16
    row_width = slab // row_count
    half = row_width // 2
    row = lax.axis_index("row")
    odd = lax.axis_index("col") % 2

    unit = total_width // sum(SHARES)
    widths = [unit * s for s in SHARES]
    starts = [sum(widths[:i]) for i in range(len(widths))]
    block = min(512, unit)

    tiles = (derivs.reshape(local, col_count, total_width), energy_derivs.reshape(local, col_count, total_width))

    slab_tiles = derivs[:, :slab].reshape(local, row_count // 2, 2 * row_width)
    tagged = energy_parts(energies)
    mine = lax.dynamic_index_in_dim(slab_tiles, row // 2, 1, keepdims=False)
    other = lax.dynamic_index_in_dim(slab_tiles, (row // 2) ^ 1, 1, keepdims=False)
    got = across(jnp.concatenate((other, tagged), axis=1), "row", 2)
    pair = (jnp.concatenate((mine, tagged), axis=1), got)

    def for_core(block_pair, core):
        return [
            jnp.concatenate(
                (lax.dynamic_slice_in_dim(b, core * row_width, row_width, 1), b[:, 2 * row_width :]), axis=1
            )
            for b in block_pair
        ]

    own_parts = for_core(pair, row % 2)
    sent = jnp.concatenate(for_core(pair, 1 - row % 2), axis=1)
    got = across(sent, "row", 1)
    piece_width = row_width + LANES
    slab_parts = own_parts + [got[:, :piece_width], got[:, piece_width:]]
    halves = [
        jnp.concatenate([jnp.concatenate((p[:, h * half : (h + 1) * half], p[:, row_width:]), axis=1) for p in slab_parts], axis=1)
        for h in range(2)
    ]
    slab_send = jnp.stack([halves[q % 2] for q in range(col_count)], axis=1)

    outs = None
    rows = shift = None
    gathered = []
    for i, (start, width) in enumerate(zip(starts, widths)):
        parts = [t[:, :, start : start + width] for t in tiles]
        if i == 1:
            parts.append(slab_send)
        swapped = lax.all_to_all(jnp.concatenate(parts, axis=2), "col", split_axis=1, concat_axis=0, tiled=True)
        swapped = swapped.reshape(local * col_count, swapped.shape[2])
        if i == 1:
            slab_got = swapped[:, 2 * width :]
            swapped = swapped[:, : 2 * width]
            tail = half + LANES
            held = jnp.concatenate([slab_got[:, q * tail : (q + 1) * tail] for q in range(4)], axis=0)
            energy = held[:, half:]
            held = held[:, :half]
            fetched = across(held, "col", 1)
            rows, shift = prepare(
                jnp.where(odd == 0, held, fetched), jnp.where(odd == 0, fetched, held), energy
            )
        far = across(swapped, "row", 2)
        gathered.append((swapped, far, across(swapped, "row", 1), across(far, "row", 1)))
    for start, width, pieces in zip(starts, widths, gathered):
        outs = chunk_products(rows, shift, pieces, start, width, block, total_width, outs)
    return tuple(outs)


def solution(mesh):
    placed = (P(("row", "col"), None), P(("row", "col"), None), P(("row", "col")))
    return jax.shard_map(
        body,
        mesh=mesh,
        in_specs=placed,
        out_specs=(P("row", "col"), P("row", "col")),
        check_vma=False,
    )
```

```python
import functools
import jax
import jax.numpy as jnp
from jax import lax
from jax.experimental import pallas as pl
from jax.experimental.pallas import tpu as pltpu
from jax.sharding import PartitionSpec as P

VMEM_BYTES = 40 * 1024 * 1024
PACK_BYTES = 58 * 1024 * 1024
LANES = 128
SHARES = (6, 7, 3)
GROUPS = ((0,), (1,), (2,))


def averaged(values, count):
    if count & (count - 1) == 0:
        return values * (1.0 / count)
    return values / count


def prepare_kernel(first_half, second_half, energy, row_out, shift_out):
    count = energy.shape[0]
    half = first_half.shape[1]
    for place, source in enumerate((first_half, second_half)):
        raw = source[...].astype(jnp.float32)
        centred = raw - averaged(jnp.sum(raw, axis=0, keepdims=True), count)
        row_out[place * half : (place + 1) * half, :] = centred.T.astype(jnp.bfloat16)
    parts = energy[...].astype(jnp.float32)
    value = (parts[:, 0:1] + parts[:, 1:2]) + parts[:, 2:3]
    shift = value - averaged(jnp.sum(value, axis=0, keepdims=True), count)
    shift_out[...] = jnp.broadcast_to(shift, shift_out.shape)


def prepare(first_half, second_half, energy):
    count, half = first_half.shape
    return pl.pallas_call(
        prepare_kernel,
        out_shape=(
            jax.ShapeDtypeStruct((2 * half, count), jnp.bfloat16),
            jax.ShapeDtypeStruct((count, LANES), jnp.float32),
        ),
        compiler_params=pltpu.CompilerParams(vmem_limit_bytes=VMEM_BYTES),
        cost_estimate=pl.CostEstimate(flops=4 * half * count, bytes_accessed=8 * half * count, transcendentals=0),
    )(first_half, second_half, energy)


def chunk_kernel(row_ref, shift_ref, *refs, pieces):
    derivs = refs[:pieces]
    grads = refs[pieces : 2 * pieces]
    correlation, hamiltonian, done = refs[-3:]
    done[...] = jnp.zeros_like(done)
    count = row_ref.shape[1]
    raw = jnp.concatenate([piece[...] for piece in derivs], axis=0).astype(jnp.float32)
    raw_grads = jnp.concatenate([piece[...] for piece in grads], axis=0).astype(jnp.float32)
    offsets = raw - averaged(jnp.sum(raw, axis=0, keepdims=True), count)
    grad_offsets = raw_grads - averaged(jnp.sum(raw_grads, axis=0, keepdims=True), count)
    centred = offsets.astype(jnp.bfloat16)
    term = (shift_ref[:, 0:1] * offsets + grad_offsets).astype(jnp.bfloat16)
    rows = row_ref[...]
    correlation[...] = averaged(jnp.dot(rows, centred, preferred_element_type=jnp.float32), count)
    hamiltonian[...] = averaged(jnp.dot(rows, term, preferred_element_type=jnp.float32), count)


def chunk_products(rows, shift, pieces, start, width, block, total_width, earlier):
    steps = width // block
    first = start // block
    n_rows = rows.shape[0]
    specs = [pl.BlockSpec(rows.shape, lambda j: (0, 0)), pl.BlockSpec(shift.shape, lambda j: (0, 0))]
    for offset in (0, steps):
        specs += [
            pl.BlockSpec((p.shape[0], block), lambda j, o=at // block + offset: (0, j + o)) for p, at in pieces
        ]
    arrays = [p for p, _ in pieces]
    operands = [rows, shift, *arrays, *arrays]
    aliases = {}
    if earlier is not None:
        aliases = {len(operands): 0, len(operands) + 1: 1}
        operands += list(earlier)
        specs += [pl.BlockSpec(memory_space=pl.ANY)] * 2
    return pl.pallas_call(
        functools.partial(chunk_kernel, pieces=len(pieces)),
        grid=(steps,),
        in_specs=specs,
        out_specs=[pl.BlockSpec((n_rows, block), lambda j: (0, j + first))] * 2
        + [pl.BlockSpec((8, LANES), lambda j: (0, 0))],
        out_shape=[jax.ShapeDtypeStruct((n_rows, total_width), jnp.float32)] * 2
        + [jax.ShapeDtypeStruct((8, LANES), jnp.float32)],
        input_output_aliases=aliases,
        compiler_params=pltpu.CompilerParams(vmem_limit_bytes=VMEM_BYTES),
        cost_estimate=pl.CostEstimate(
            flops=4 * n_rows * width * rows.shape[1], bytes_accessed=8 * n_rows * width, transcendentals=0
        ),
    )(*operands)


def pack_kernel(energy_ref, slab_ref, derivs_ref, grads_ref, *outs, peers, groups, tile, slab, rows):
    local = derivs_ref.shape[0]
    half = slab // (2 * rows)
    place = lax.broadcasted_iota(jnp.int32, (local, LANES), 0)
    lane = lax.broadcasted_iota(jnp.int32, (local, LANES), 1)
    value = jnp.zeros((local, LANES), jnp.float32)
    for sample in range(local):
        value = jnp.where(place == sample, energy_ref[sample], value)
    high = value.astype(jnp.bfloat16).astype(jnp.float32)
    rest = value - high
    middle = rest.astype(jnp.bfloat16).astype(jnp.float32)
    low = rest - middle
    tag = jnp.where(lane == 0, high, jnp.where(lane == 1, middle, jnp.where(lane == 2, low, 0.0)))
    tag = tag.astype(jnp.bfloat16)
    for number, (out, group) in enumerate(zip(outs, groups)):
        width = out.shape[1] // peers
        for peer in range(peers):
            at = peer * width
            for begin, end in group:
                for source in (derivs_ref, grads_ref):
                    out[:, at : at + end - begin] = source[:, peer * tile + begin : peer * tile + end]
                    at += end - begin
            if number == 0:
                for row in range(rows):
                    begin = (2 * row + peer % 2) * half
                    out[:, at : at + half] = slab_ref[:, begin : begin + half]
                    at += half
                out[:, at : at + LANES] = tag


def pack(energies, derivs, grads, peers, groups, slab, rows):
    local, width = derivs.shape
    tile = width // peers
    widths = [2 * sum(end - begin for begin, end in group) for group in groups]
    widths[0] += slab // 2 + LANES
    return pl.pallas_call(
        functools.partial(pack_kernel, peers=2, groups=groups, tile=tile, slab=slab, rows=rows),
        grid=(peers // 2,),
        in_specs=[
            pl.BlockSpec(memory_space=pltpu.SMEM),
            pl.BlockSpec((local, slab), lambda j: (0, 0)),
            pl.BlockSpec((local, 2 * tile), lambda j: (0, j)),
            pl.BlockSpec((local, 2 * tile), lambda j: (0, j)),
        ],
        out_specs=[pl.BlockSpec((local, 2 * w), lambda j: (0, j)) for w in widths],
        out_shape=[jax.ShapeDtypeStruct((local, peers * w), derivs.dtype) for w in widths],
        compiler_params=pltpu.CompilerParams(vmem_limit_bytes=PACK_BYTES),
    )(energies, derivs, derivs, grads)


def across(value, axis, distance):
    size = lax.axis_size(axis)
    return lax.ppermute(value, axis, [(i, i ^ distance) for i in range(size)])


def tied(value, *others):
    return lax.optimization_barrier((value, *others))[0]


def body(derivs, energy_derivs, energies):
    row_count = lax.axis_size("row")
    col_count = lax.axis_size("col")
    local = derivs.shape[0]
    total_width = derivs.shape[1] // col_count
    slab = derivs.shape[1] // 16
    row_width = slab // row_count
    half = row_width // 2
    row = lax.axis_index("row")
    odd = lax.axis_index("col") % 2

    unit = total_width // sum(SHARES)
    widths = [unit * s for s in SHARES]
    starts = [sum(widths[:i]) for i in range(len(widths))]
    block = min(512, unit)

    def to_owners(value):
        width = value.shape[1] // col_count
        tiles = value.reshape(value.shape[0], col_count, width)
        got = lax.all_to_all(tiles, "col", split_axis=1, concat_axis=0, tiled=True)
        return got.reshape(value.shape[0] * col_count, width)

    def take(value, index, width):
        return lax.dynamic_slice_in_dim(value, index * width, width, 1)

    def slab_pair(got):
        values, tags = got[:, : slab // 2], got[:, slab // 2 :]
        mine = jnp.concatenate((take(values, row // 2, 2 * half), tags), axis=1)
        sent = jnp.concatenate((take(values, 1 - row // 2, 2 * half), tags), axis=1)
        return jnp.concatenate((mine, across(sent, "row", 2)), axis=0)

    def slab_columns(pair):
        values, tags = pair[:, : 2 * half], pair[:, 2 * half :]
        mine = jnp.concatenate((take(values, row % 2, half), tags), axis=1)
        sent = jnp.concatenate((take(values, 1 - row % 2, half), tags), axis=1)
        quad = jnp.concatenate((mine, across(sent, "row", 1)), axis=0)
        return quad[:, :half], quad[:, half:]

    def slab_rows(held, tags):
        fetched = across(held, "col", 1)
        return prepare(jnp.where(odd == 0, held, fetched), jnp.where(odd == 0, fetched, held), tags)

    def products(i, pieces, outs):
        return chunk_products(rows, shift, pieces, starts[i], widths[i], block, total_width, outs)

    cuts = [(begin, begin + width) for begin, width in zip(starts, widths)]
    groups = [[cuts[i] for i in group] for group in GROUPS]
    sends = pack(energies, derivs, energy_derivs, col_count, groups, slab, row_count)
    last = len(widths) - 1
    wide = 2 * widths[last]
    last_far = across(sends[-1], "row", 2)
    joined = jnp.concatenate(
        (sends[-1].reshape(local, col_count, wide), last_far.reshape(local, col_count, wide)), axis=2
    )
    near, far = {}, {}

    def split(got, group):
        at = 0
        for i in group:
            near[i] = got[:, at : at + 2 * widths[i]]
            at += 2 * widths[i]
        return got[:, at:]

    first, joined = lax.optimization_barrier((to_owners(sends[0]), joined))
    pair = slab_pair(split(first, GROUPS[0]))
    held, tags = slab_columns(pair)
    rows, shift = slab_rows(held, tags)
    far[0] = tied(across(near[0], "row", 2), rows)
    for i in GROUPS[0][1:]:
        far[i] = across(near[i], "row", 2)
    for send, group in zip(sends[1:-1], GROUPS[1:-1]):
        split(to_owners(send), group)
        for i in group:
            far[i] = across(near[i], "row", 2)
    joined = joined.reshape(local, -1)
    joined = tied(joined, rows)
    ends = to_owners(joined)
    outs = done = None
    for i in range(len(widths)):
        if i == last:
            ends = tied(ends, begun)
            other = across(ends, "row", 1)
            pieces = [(ends, 0), (ends, wide), (other, 0), (other, wide)]
        else:
            if done is not None:
                far[i] = tied(far[i], done)
            pieces = [(near[i], 0), (far[i], 0), (across(near[i], "row", 1), 0), (across(far[i], "row", 1), 0)]
        *outs, done = products(i, pieces, outs)
        if i == 0:
            begun = done
    return tuple(outs)


def solution(mesh):
    placed = (P(("row", "col"), None), P(("row", "col"), None), P(("row", "col")))
    return jax.shard_map(
        body,
        mesh=mesh,
        in_specs=placed,
        out_specs=(P("row", "col"), P("row", "col")),
        check_vma=False,
    )
```

```python
import functools
import jax
import jax.numpy as jnp
from jax import lax
from jax.experimental import pallas as pl
from jax.experimental.pallas import tpu as pltpu
from jax.sharding import PartitionSpec as P

VMEM_BYTES = 40 * 1024 * 1024
PACK_BYTES = 58 * 1024 * 1024
LANES = 128
PACKED = 4
SHARES = (6, 7, 3)
GROUPS = ((0,), (1,), (2,))


def averaged(values, count):
    if count & (count - 1) == 0:
        return values * (1.0 / count)
    return values / count


def prepare_kernel(first_half, second_half, energy, row_out, shift_out):
    count = energy.shape[0]
    half = first_half.shape[1]
    for place, source in enumerate((first_half, second_half)):
        raw = source[...].astype(jnp.float32)
        centred = raw - averaged(jnp.sum(raw, axis=0, keepdims=True), count)
        row_out[place * half : (place + 1) * half, :] = centred.T.astype(jnp.bfloat16)
    parts = energy[...].astype(jnp.float32)
    value = (parts[:, 0:1] + parts[:, 1:2]) + parts[:, 2:3]
    shift = value - averaged(jnp.sum(value, axis=0, keepdims=True), count)
    shift_out[...] = jnp.broadcast_to(shift, shift_out.shape)


def prepare(first_half, second_half, energy):
    count, half = first_half.shape
    return pl.pallas_call(
        prepare_kernel,
        out_shape=(
            jax.ShapeDtypeStruct((2 * half, count), jnp.bfloat16),
            jax.ShapeDtypeStruct((count, LANES), jnp.float32),
        ),
        compiler_params=pltpu.CompilerParams(vmem_limit_bytes=VMEM_BYTES),
        cost_estimate=pl.CostEstimate(flops=4 * half * count, bytes_accessed=8 * half * count, transcendentals=0),
    )(first_half, second_half, energy)


def chunk_kernel(row_ref, shift_ref, *refs, pieces):
    derivs = refs[:pieces]
    grads = refs[pieces : 2 * pieces]
    correlation, hamiltonian, done = refs[-3:]
    done[...] = jnp.zeros_like(done)
    count = row_ref.shape[1]
    raw = jnp.concatenate([piece[...] for piece in derivs], axis=0).astype(jnp.float32)
    raw_grads = jnp.concatenate([piece[...] for piece in grads], axis=0).astype(jnp.float32)
    offsets = raw - averaged(jnp.sum(raw, axis=0, keepdims=True), count)
    grad_offsets = raw_grads - averaged(jnp.sum(raw_grads, axis=0, keepdims=True), count)
    centred = offsets.astype(jnp.bfloat16)
    term = (shift_ref[:, 0:1] * offsets + grad_offsets).astype(jnp.bfloat16)
    rows = row_ref[...]
    correlation[...] = averaged(jnp.dot(rows, centred, preferred_element_type=jnp.float32), count)
    hamiltonian[...] = averaged(jnp.dot(rows, term, preferred_element_type=jnp.float32), count)


def chunk_products(rows, shift, pieces, start, width, block, total_width, earlier):
    steps = width // block
    first = start // block
    n_rows = rows.shape[0]
    specs = [pl.BlockSpec(rows.shape, lambda j: (0, 0)), pl.BlockSpec(shift.shape, lambda j: (0, 0))]
    for offset in (0, steps):
        specs += [
            pl.BlockSpec((p.shape[0], block), lambda j, o=at // block + offset: (0, j + o)) for p, at in pieces
        ]
    arrays = [p for p, _ in pieces]
    operands = [rows, shift, *arrays, *arrays]
    aliases = {}
    if earlier is not None:
        aliases = {len(operands): 0, len(operands) + 1: 1}
        operands += list(earlier)
        specs += [pl.BlockSpec(memory_space=pl.ANY)] * 2
    return pl.pallas_call(
        functools.partial(chunk_kernel, pieces=len(pieces)),
        grid=(steps,),
        in_specs=specs,
        out_specs=[pl.BlockSpec((n_rows, block), lambda j: (0, j + first))] * 2
        + [pl.BlockSpec((8, LANES), lambda j: (0, 0))],
        out_shape=[jax.ShapeDtypeStruct((n_rows, total_width), jnp.float32)] * 2
        + [jax.ShapeDtypeStruct((8, LANES), jnp.float32)],
        input_output_aliases=aliases,
        compiler_params=pltpu.CompilerParams(vmem_limit_bytes=VMEM_BYTES),
        cost_estimate=pl.CostEstimate(
            flops=4 * n_rows * width * rows.shape[1], bytes_accessed=8 * n_rows * width, transcendentals=0
        ),
    )(*operands)


def pack_kernel(energy_ref, slab_ref, derivs_ref, grads_ref, *outs, peers, groups, tile, slab, rows):
    local = derivs_ref.shape[0]
    half = slab // (2 * rows)
    place = lax.broadcasted_iota(jnp.int32, (local, LANES), 0)
    lane = lax.broadcasted_iota(jnp.int32, (local, LANES), 1)
    value = jnp.zeros((local, LANES), jnp.float32)
    for sample in range(local):
        value = jnp.where(place == sample, energy_ref[sample], value)
    high = value.astype(jnp.bfloat16).astype(jnp.float32)
    rest = value - high
    middle = rest.astype(jnp.bfloat16).astype(jnp.float32)
    low = rest - middle
    tag = jnp.where(lane == 0, high, jnp.where(lane == 1, middle, jnp.where(lane == 2, low, 0.0)))
    tag = tag.astype(jnp.bfloat16)
    for number, (out, group) in enumerate(zip(outs, groups)):
        width = out.shape[1] // peers
        for peer in range(peers):
            at = peer * width
            for begin, end in group:
                for source in (derivs_ref, grads_ref):
                    out[:, at : at + end - begin] = source[:, peer * tile + begin : peer * tile + end]
                    at += end - begin
            if number == 0:
                for row in range(rows):
                    begin = (2 * row + peer % 2) * half
                    out[:, at : at + half] = slab_ref[:, begin : begin + half]
                    at += half
                out[:, at : at + LANES] = tag


def pack(energies, derivs, grads, peers, groups, slab, rows):
    local, width = derivs.shape
    tile = width // peers
    widths = [2 * sum(end - begin for begin, end in group) for group in groups]
    widths[0] += slab // 2 + LANES
    return pl.pallas_call(
        functools.partial(pack_kernel, peers=PACKED, groups=groups, tile=tile, slab=slab, rows=rows),
        grid=(peers // PACKED,),
        in_specs=[
            pl.BlockSpec(memory_space=pltpu.SMEM),
            pl.BlockSpec((local, slab), lambda j: (0, 0)),
            pl.BlockSpec((local, PACKED * tile), lambda j: (0, j)),
            pl.BlockSpec((local, PACKED * tile), lambda j: (0, j)),
        ],
        out_specs=[pl.BlockSpec((local, PACKED * w), lambda j: (0, j)) for w in widths],
        out_shape=[jax.ShapeDtypeStruct((local, peers * w), derivs.dtype) for w in widths],
        compiler_params=pltpu.CompilerParams(vmem_limit_bytes=PACK_BYTES),
    )(energies, derivs, derivs, grads)


def across(value, axis, distance):
    size = lax.axis_size(axis)
    return lax.ppermute(value, axis, [(i, i ^ distance) for i in range(size)])


def tied(value, *others):
    return lax.optimization_barrier((value, *others))[0]


def body(derivs, energy_derivs, energies):
    row_count = lax.axis_size("row")
    col_count = lax.axis_size("col")
    local = derivs.shape[0]
    total_width = derivs.shape[1] // col_count
    slab = derivs.shape[1] // 16
    row_width = slab // row_count
    half = row_width // 2
    row = lax.axis_index("row")
    odd = lax.axis_index("col") % 2

    unit = total_width // sum(SHARES)
    widths = [unit * s for s in SHARES]
    starts = [sum(widths[:i]) for i in range(len(widths))]
    block = min(512, unit)

    def to_owners(value):
        width = value.shape[1] // col_count
        tiles = value.reshape(value.shape[0], col_count, width)
        got = lax.all_to_all(tiles, "col", split_axis=1, concat_axis=0, tiled=True)
        return got.reshape(value.shape[0] * col_count, width)

    def take(value, index, width):
        return lax.dynamic_slice_in_dim(value, index * width, width, 1)

    def slab_pair(got):
        values, tags = got[:, : slab // 2], got[:, slab // 2 :]
        mine = jnp.concatenate((take(values, row // 2, 2 * half), tags), axis=1)
        sent = jnp.concatenate((take(values, 1 - row // 2, 2 * half), tags), axis=1)
        return jnp.concatenate((mine, across(sent, "row", 2)), axis=0)

    def slab_columns(pair):
        values, tags = pair[:, : 2 * half], pair[:, 2 * half :]
        mine = jnp.concatenate((take(values, row % 2, half), tags), axis=1)
        sent = jnp.concatenate((take(values, 1 - row % 2, half), tags), axis=1)
        quad = jnp.concatenate((mine, across(sent, "row", 1)), axis=0)
        return quad[:, :half], quad[:, half:]

    def slab_rows(held, tags):
        fetched = across(held, "col", 1)
        return prepare(jnp.where(odd == 0, held, fetched), jnp.where(odd == 0, fetched, held), tags)

    def products(i, pieces, outs):
        return chunk_products(rows, shift, pieces, starts[i], widths[i], block, total_width, outs)

    cuts = [(begin, begin + width) for begin, width in zip(starts, widths)]
    groups = [[cuts[i] for i in group] for group in GROUPS]
    sends = pack(energies, derivs, energy_derivs, col_count, groups, slab, row_count)
    last = len(widths) - 1
    wide = 2 * widths[last]
    last_far = across(sends[-1], "row", 2)
    joined = jnp.concatenate(
        (sends[-1].reshape(local, col_count, wide), last_far.reshape(local, col_count, wide)), axis=2
    )
    near, far = {}, {}

    def split(got, group):
        at = 0
        for i in group:
            near[i] = got[:, at : at + 2 * widths[i]]
            at += 2 * widths[i]
        return got[:, at:]

    first, joined = lax.optimization_barrier((to_owners(sends[0]), joined))
    pair = slab_pair(split(first, GROUPS[0]))
    held, tags = slab_columns(pair)
    rows, shift = slab_rows(held, tags)
    far[0] = tied(across(near[0], "row", 2), rows)
    for i in GROUPS[0][1:]:
        far[i] = across(near[i], "row", 2)
    for send, group in zip(sends[1:-1], GROUPS[1:-1]):
        split(to_owners(send), group)
        for i in group:
            far[i] = across(near[i], "row", 2)
    joined = joined.reshape(local, -1)
    joined = tied(joined, rows)
    ends = to_owners(joined)
    outs = done = None
    for i in range(len(widths)):
        if i == last:
            ends = tied(ends, begun)
            other = across(ends, "row", 1)
            pieces = [(ends, 0), (ends, wide), (other, 0), (other, wide)]
        else:
            if done is not None:
                far[i] = tied(far[i], done)
            pieces = [(near[i], 0), (far[i], 0), (across(near[i], "row", 1), 0), (across(far[i], "row", 1), 0)]
        *outs, done = products(i, pieces, outs)
        if i == 0:
            begun = done
    return tuple(outs)


def solution(mesh):
    placed = (P(("row", "col"), None), P(("row", "col"), None), P(("row", "col")))
    return jax.shard_map(
        body,
        mesh=mesh,
        in_specs=placed,
        out_specs=(P("row", "col"), P("row", "col")),
        check_vma=False,
    )
```

```python
import functools
import jax
import jax.numpy as jnp
from jax import lax
from jax.experimental import pallas as pl
from jax.experimental.pallas import tpu as pltpu
from jax.sharding import PartitionSpec as P

VMEM_BYTES = 40 * 1024 * 1024
PACK_BYTES = 58 * 1024 * 1024
LANES = 128
PACKED = 4
SHARES = (7, 7, 2)
GROUPS = ((0,), (1,), (2,))


def averaged(values, count):
    if count & (count - 1) == 0:
        return values * (1.0 / count)
    return values / count


def prepare_kernel(first_half, second_half, energy, row_out, shift_out):
    count = energy.shape[0]
    half = first_half.shape[1]
    for place, source in enumerate((first_half, second_half)):
        raw = source[...].astype(jnp.float32)
        centred = raw - averaged(jnp.sum(raw, axis=0, keepdims=True), count)
        row_out[place * half : (place + 1) * half, :] = centred.T.astype(jnp.bfloat16)
    parts = energy[...].astype(jnp.float32)
    value = (parts[:, 0:1] + parts[:, 1:2]) + parts[:, 2:3]
    shift = value - averaged(jnp.sum(value, axis=0, keepdims=True), count)
    shift_out[...] = jnp.broadcast_to(shift, shift_out.shape)


def prepare(first_half, second_half, energy):
    count, half = first_half.shape
    return pl.pallas_call(
        prepare_kernel,
        out_shape=(
            jax.ShapeDtypeStruct((2 * half, count), jnp.bfloat16),
            jax.ShapeDtypeStruct((count, LANES), jnp.float32),
        ),
        compiler_params=pltpu.CompilerParams(vmem_limit_bytes=VMEM_BYTES),
        cost_estimate=pl.CostEstimate(flops=4 * half * count, bytes_accessed=8 * half * count, transcendentals=0),
    )(first_half, second_half, energy)


def chunk_kernel(row_ref, shift_ref, *refs, pieces):
    derivs = refs[:pieces]
    grads = refs[pieces : 2 * pieces]
    correlation, hamiltonian, done = refs[-3:]
    done[...] = jnp.zeros_like(done)
    count = row_ref.shape[1]
    raw = jnp.concatenate([piece[...] for piece in derivs], axis=0).astype(jnp.float32)
    raw_grads = jnp.concatenate([piece[...] for piece in grads], axis=0).astype(jnp.float32)
    offsets = raw - averaged(jnp.sum(raw, axis=0, keepdims=True), count)
    grad_offsets = raw_grads - averaged(jnp.sum(raw_grads, axis=0, keepdims=True), count)
    centred = offsets.astype(jnp.bfloat16)
    term = (shift_ref[:, 0:1] * offsets + grad_offsets).astype(jnp.bfloat16)
    rows = row_ref[...]
    correlation[...] = averaged(jnp.dot(rows, centred, preferred_element_type=jnp.float32), count)
    hamiltonian[...] = averaged(jnp.dot(rows, term, preferred_element_type=jnp.float32), count)


def chunk_products(rows, shift, pieces, start, width, block, total_width, earlier):
    steps = width // block
    first = start // block
    n_rows = rows.shape[0]
    specs = [pl.BlockSpec(rows.shape, lambda j: (0, 0)), pl.BlockSpec(shift.shape, lambda j: (0, 0))]
    for offset in (0, steps):
        specs += [
            pl.BlockSpec((p.shape[0], block), lambda j, o=at // block + offset: (0, j + o)) for p, at in pieces
        ]
    arrays = [p for p, _ in pieces]
    operands = [rows, shift, *arrays, *arrays]
    aliases = {}
    if earlier is not None:
        aliases = {len(operands): 0, len(operands) + 1: 1}
        operands += list(earlier)
        specs += [pl.BlockSpec(memory_space=pl.ANY)] * 2
    return pl.pallas_call(
        functools.partial(chunk_kernel, pieces=len(pieces)),
        grid=(steps,),
        in_specs=specs,
        out_specs=[pl.BlockSpec((n_rows, block), lambda j: (0, j + first))] * 2
        + [pl.BlockSpec((8, LANES), lambda j: (0, 0))],
        out_shape=[jax.ShapeDtypeStruct((n_rows, total_width), jnp.float32)] * 2
        + [jax.ShapeDtypeStruct((8, LANES), jnp.float32)],
        input_output_aliases=aliases,
        compiler_params=pltpu.CompilerParams(vmem_limit_bytes=VMEM_BYTES),
        cost_estimate=pl.CostEstimate(
            flops=4 * n_rows * width * rows.shape[1], bytes_accessed=8 * n_rows * width, transcendentals=0
        ),
    )(*operands)


def pack_kernel(energy_ref, slab_ref, derivs_ref, grads_ref, *outs, peers, groups, tile, slab, rows):
    local = derivs_ref.shape[0]
    half = slab // (2 * rows)
    place = lax.broadcasted_iota(jnp.int32, (local, LANES), 0)
    lane = lax.broadcasted_iota(jnp.int32, (local, LANES), 1)
    value = jnp.zeros((local, LANES), jnp.float32)
    for sample in range(local):
        value = jnp.where(place == sample, energy_ref[sample], value)
    high = value.astype(jnp.bfloat16).astype(jnp.float32)
    rest = value - high
    middle = rest.astype(jnp.bfloat16).astype(jnp.float32)
    low = rest - middle
    tag = jnp.where(lane == 0, high, jnp.where(lane == 1, middle, jnp.where(lane == 2, low, 0.0)))
    tag = tag.astype(jnp.bfloat16)
    for number, (out, group) in enumerate(zip(outs, groups)):
        width = out.shape[1] // peers
        for peer in range(peers):
            at = peer * width
            for begin, end in group:
                for source in (derivs_ref, grads_ref):
                    out[:, at : at + end - begin] = source[:, peer * tile + begin : peer * tile + end]
                    at += end - begin
            if number == 0:
                for row in range(rows):
                    begin = (2 * row + peer % 2) * half
                    out[:, at : at + half] = slab_ref[:, begin : begin + half]
                    at += half
                out[:, at : at + LANES] = tag


def pack(energies, derivs, grads, peers, groups, slab, rows):
    local, width = derivs.shape
    tile = width // peers
    widths = [2 * sum(end - begin for begin, end in group) for group in groups]
    widths[0] += slab // 2 + LANES
    return pl.pallas_call(
        functools.partial(pack_kernel, peers=PACKED, groups=groups, tile=tile, slab=slab, rows=rows),
        grid=(peers // PACKED,),
        in_specs=[
            pl.BlockSpec(memory_space=pltpu.SMEM),
            pl.BlockSpec((local, slab), lambda j: (0, 0)),
            pl.BlockSpec((local, PACKED * tile), lambda j: (0, j)),
            pl.BlockSpec((local, PACKED * tile), lambda j: (0, j)),
        ],
        out_specs=[pl.BlockSpec((local, PACKED * w), lambda j: (0, j)) for w in widths],
        out_shape=[jax.ShapeDtypeStruct((local, peers * w), derivs.dtype) for w in widths],
        compiler_params=pltpu.CompilerParams(vmem_limit_bytes=PACK_BYTES),
    )(energies, derivs, derivs, grads)


def across(value, axis, distance):
    size = lax.axis_size(axis)
    return lax.ppermute(value, axis, [(i, i ^ distance) for i in range(size)])


def tied(value, *others):
    return lax.optimization_barrier((value, *others))[0]


def body(derivs, energy_derivs, energies):
    row_count = lax.axis_size("row")
    col_count = lax.axis_size("col")
    local = derivs.shape[0]
    total_width = derivs.shape[1] // col_count
    slab = derivs.shape[1] // 16
    row_width = slab // row_count
    half = row_width // 2
    row = lax.axis_index("row")
    odd = lax.axis_index("col") % 2

    unit = total_width // sum(SHARES)
    widths = [unit * s for s in SHARES]
    starts = [sum(widths[:i]) for i in range(len(widths))]
    block = min(512, unit)

    def to_owners(value):
        width = value.shape[1] // col_count
        tiles = value.reshape(value.shape[0], col_count, width)
        got = lax.all_to_all(tiles, "col", split_axis=1, concat_axis=0, tiled=True)
        return got.reshape(value.shape[0] * col_count, width)

    def take(value, index, width):
        return lax.dynamic_slice_in_dim(value, index * width, width, 1)

    def slab_pair(got):
        values, tags = got[:, : slab // 2], got[:, slab // 2 :]
        mine = jnp.concatenate((take(values, row // 2, 2 * half), tags), axis=1)
        sent = jnp.concatenate((take(values, 1 - row // 2, 2 * half), tags), axis=1)
        return jnp.concatenate((mine, across(sent, "row", 2)), axis=0)

    def slab_columns(pair):
        values, tags = pair[:, : 2 * half], pair[:, 2 * half :]
        mine = jnp.concatenate((take(values, row % 2, half), tags), axis=1)
        sent = jnp.concatenate((take(values, 1 - row % 2, half), tags), axis=1)
        quad = jnp.concatenate((mine, across(sent, "row", 1)), axis=0)
        return quad[:, :half], quad[:, half:]

    def slab_rows(held, tags):
        fetched = across(held, "col", 1)
        return prepare(jnp.where(odd == 0, held, fetched), jnp.where(odd == 0, fetched, held), tags)

    def products(i, pieces, outs):
        return chunk_products(rows, shift, pieces, starts[i], widths[i], block, total_width, outs)

    cuts = [(begin, begin + width) for begin, width in zip(starts, widths)]
    groups = [[cuts[i] for i in group] for group in GROUPS]
    sends = pack(energies, derivs, energy_derivs, col_count, groups, slab, row_count)
    last = len(widths) - 1
    wide = 2 * widths[last]
    last_far = across(sends[-1], "row", 2)
    joined = jnp.concatenate(
        (sends[-1].reshape(local, col_count, wide), last_far.reshape(local, col_count, wide)), axis=2
    )
    near, far = {}, {}

    def split(got, group):
        at = 0
        for i in group:
            near[i] = got[:, at : at + 2 * widths[i]]
            at += 2 * widths[i]
        return got[:, at:]

    first, joined = lax.optimization_barrier((to_owners(sends[0]), joined))
    pair = slab_pair(split(first, GROUPS[0]))
    held, tags = slab_columns(pair)
    rows, shift = slab_rows(held, tags)
    far[0] = tied(across(near[0], "row", 2), rows)
    for i in GROUPS[0][1:]:
        far[i] = across(near[i], "row", 2)
    for send, group in zip(sends[1:-1], GROUPS[1:-1]):
        split(to_owners(send), group)
        for i in group:
            far[i] = across(near[i], "row", 2)
    joined = joined.reshape(local, -1)
    joined = tied(joined, rows)
    ends = to_owners(joined)
    outs = done = None
    for i in range(len(widths)):
        if i == last:
            ends = tied(ends, begun)
            other = across(ends, "row", 1)
            pieces = [(ends, 0), (ends, wide), (other, 0), (other, wide)]
        else:
            if done is not None:
                far[i] = tied(far[i], done)
            pieces = [(near[i], 0), (far[i], 0), (across(near[i], "row", 1), 0), (across(far[i], "row", 1), 0)]
        *outs, done = products(i, pieces, outs)
        if i == 0:
            begun = done
    return tuple(outs)


def solution(mesh):
    placed = (P(("row", "col"), None), P(("row", "col"), None), P(("row", "col")))
    return jax.shard_map(
        body,
        mesh=mesh,
        in_specs=placed,
        out_specs=(P("row", "col"), P("row", "col")),
        check_vma=False,
    )
```
